32 devices in a mesh: gx: 4 (over y, x), gy: 2 (over core), sa: 4 (over z).
Axes of the slice: x: 2, y: 2, z: 4, core: 2. Of those that a mesh axis runs over, the one named last changes fastest.
Arguments:
- pixels: bfloat16 [16, 512, 8192], P('sa', 'gy', 'gx'), may hold values from -6 to 6
- peak_offsets: int32 [16, 2, 8, 128], P('sa', None, 'gy', 'gx'), may hold values from -2 to 2
- validity: int32 [16, 8, 128], P('sa', 'gy', 'gx'), may hold values 0 or 1
Outputs:
- flow_field: float32 [16, 2, 8, 128], P('sa', None, 'gy', 'gx')
- mesh_field: float32 [16, 2, 8, 128], P('sa', None, 'gy', 'gx')
The draws below stay inside these ranges and needn't reach their ends.
All inputs are finite; a program needn't handle non-finite values. No bound on the sum of `validity` on one device may be relied on, other than what follows from the above.
Results may differ from the reference program's by a relative error of at most 0.0035.
Values may be sent and summed in bfloat16 or wider, within the bound.
A program may use at most 192 MiB of HBM per device.

```python
import math
import jax
import jax.numpy as jnp
from jax import lax

PATCH = 64
RELAX = 8
SECTIONS = 16
ROWS = 512
COLS = 8192
NR = 8
NC = 128


def plant(array, rng, smallest, high):
    index_at = [jax.random.randint(jax.random.fold_in(rng, axis), (), 0, length) for axis, length in enumerate(array.shape)]
    main_axis = array.shape.index(max(array.shape))
    next_to = index_at[:main_axis] + [(index_at[main_axis] + 1) % array.shape[main_axis]] + index_at[main_axis + 1:]
    return array.at[tuple(index_at)].set(smallest).at[tuple(next_to)].set(high)


def steps_of(stream_key, shape, pieces, least, largest):
    loudness, own = 1.0, jax.random.fold_in(stream_key, 6)
    for axis_at, blocks in pieces:
        draws = jnp.exp(jax.random.uniform(jax.random.fold_in(own, axis_at), (blocks,), jnp.float32, least / len(pieces), largest / len(pieces)))
        loudness = loudness * jnp.repeat(draws, shape[axis_at] // blocks).reshape([-1 if axis == axis_at else 1 for axis in range(len(shape))])
    return loudness


def gaussian(stream_key, extent, width, reach, pieces=(), kind=jnp.bfloat16):
    result = width * jax.random.normal(stream_key, extent, jnp.float32)
    if pieces:
        result = result * steps_of(stream_key, extent, pieces, -0.22, 0.18)
    return jnp.clip(result, -reach, reach).astype(kind)


def setup_inputs(seed: int = 0) -> dict:
    splits = jax.random.split(jax.random.key(seed), 4)
    pixels = gaussian(splits[0], (SECTIONS, ROWS, COLS), 1.0, 6.0, ((0, 4), (1, 2), (2, 4)))
    peak_offsets = plant(jax.random.randint(splits[1], (SECTIONS, 2, NR, NC), -2, 3), jax.random.fold_in(splits[1], 1), -2, 2).astype(jnp.int32)
    validity = plant((jax.random.randint(splits[2], (SECTIONS, NR, NC), 0, 4) < 3).astype(jnp.int32), jax.random.fold_in(splits[2], 1), 0, 1)
    return dict(pixels=pixels, peak_offsets=peak_offsets, validity=validity)


spring_plane = 0.5
spring_stack = 1.0
step_size = 0.2
damping = 0.6
whiten_floor = 1024.0

def to_half(values):
    return lax.optimization_barrier(values.astype(jnp.bfloat16)).astype(jnp.float32)

def dft_tables():
    frequency = jnp.arange(PATCH, dtype=jnp.int32)
    phases = frequency[:, None] * frequency[None, :] % PATCH
    angles = phases.astype(jnp.float32) * (2.0 * math.pi / PATCH)
    return (to_half(jnp.cos(angles)), to_half(jnp.sin(angles)))

def strip_spectrum(strip):
    cosine, sine_table = dft_tables()
    blocks = strip.astype(jnp.float32).reshape(PATCH, -1, PATCH)
    col_real = to_half(jnp.einsum('xbj,jk->xbk', blocks, cosine))
    col_imag = to_half(-jnp.einsum('xbj,jk->xbk', blocks, sine_table))
    spec_real = jnp.einsum('kx,xbj->kbj', cosine, col_real) + jnp.einsum('kx,xbj->kbj', sine_table, col_imag)
    spec_imag = jnp.einsum('kx,xbj->kbj', cosine, col_imag) - jnp.einsum('kx,xbj->kbj', sine_table, col_real)
    return (spec_real.astype(jnp.bfloat16), spec_imag.astype(jnp.bfloat16))

def phase_tables(offsets):
    frequency = jnp.arange(PATCH, dtype=jnp.int32)
    nearby = jnp.arange(3, dtype=jnp.int32) - 1
    phases = frequency[None, :, None] * (offsets[:, None, None] + nearby[None, None, :]) % PATCH
    angles = phases.astype(jnp.float32) * (2.0 * math.pi / PATCH)
    return (to_half(jnp.cos(angles)), to_half(jnp.sin(angles)))

def subpixel(correlation, offsets):
    center = correlation[..., 1, 1]
    row_low = correlation[..., 0, 1]
    row_high = correlation[..., 2, 1]
    col_low = correlation[..., 1, 0]
    col_high = correlation[..., 1, 2]
    row_step = (row_low - row_high) / (2.0 * jnp.maximum(jnp.abs(row_low - 2.0 * center + row_high), 1.0))
    col_step = (col_low - col_high) / (2.0 * jnp.maximum(jnp.abs(col_low - 2.0 * center + col_high), 1.0))
    return jnp.stack([offsets[0].astype(jnp.float32) + row_step, offsets[1].astype(jnp.float32) + col_step], 0)

def refine(current, previous, offsets):
    now_real = current[0].astype(jnp.float32)
    now_imag = current[1].astype(jnp.float32)
    old_real = previous[0].astype(jnp.float32)
    old_imag = previous[1].astype(jnp.float32)
    cross_real = now_real * old_real + now_imag * old_imag
    cross_imag = now_imag * old_real - now_real * old_imag
    scale = jnp.sqrt(cross_real * cross_real + cross_imag * cross_imag + whiten_floor * whiten_floor)
    prod_real = to_half(cross_real / scale)
    prod_imag = to_half(cross_imag / scale)
    col_cos, col_sin = phase_tables(offsets[1])
    row_cos, row_sin = phase_tables(offsets[0])
    high = lax.Precision.HIGHEST
    half_real = to_half(jnp.einsum('kbj,bjd->kbd', prod_real, col_cos, precision=high) - jnp.einsum('kbj,bjd->kbd', prod_imag, col_sin, precision=high))
    half_imag = to_half(jnp.einsum('kbj,bjd->kbd', prod_real, col_sin, precision=high) + jnp.einsum('kbj,bjd->kbd', prod_imag, col_cos, precision=high))
    correlation = (jnp.einsum('kbd,bke->bed', half_real, row_cos, precision=high) - jnp.einsum('kbd,bke->bed', half_imag, row_sin, precision=high)) / float(PATCH)
    return subpixel(correlation, offsets)

def relax(flow_field, validity):
    weight = validity.astype(jnp.float32)[:, None]
    mesh_state = jnp.cumsum(flow_field, axis=0)
    weight_next = jnp.concatenate([weight[1:], jnp.zeros_like(weight[:1])], 0)
    flow_next = jnp.concatenate([flow_field[1:], jnp.zeros_like(flow_field[:1])], 0)
    row_index = jnp.arange(NR, dtype=jnp.int32)[:, None]
    col_index = jnp.arange(NC, dtype=jnp.int32)[None, :]
    degree = 4.0 - (row_index == 0).astype(jnp.float32) - (row_index == NR - 1).astype(jnp.float32) - (col_index == 0).astype(jnp.float32) - (col_index == NC - 1).astype(jnp.float32)
    velocity = jnp.zeros_like(mesh_state)
    for iteration in range(RELAX):
        padded = jnp.pad(mesh_state, ((1, 1), (0, 0), (1, 1), (1, 1)))
        neighbours = padded[1:-1, :, :-2, 1:-1] + padded[1:-1, :, 2:, 1:-1] + padded[1:-1, :, 1:-1, :-2] + padded[1:-1, :, 1:-1, 2:]
        lower_mesh = padded[:-2, :, 1:-1, 1:-1]
        upper_mesh = padded[2:, :, 1:-1, 1:-1]
        here_term = weight * (mesh_state - lower_mesh - flow_field)
        next_term = weight_next * (upper_mesh - mesh_state - flow_next)
        gradient = spring_plane * (degree * mesh_state - neighbours) + spring_stack * (here_term - next_term)
        velocity = damping * velocity - step_size * gradient
        mesh_state = mesh_state + velocity
    return mesh_state

def reference(pixels, peak_offsets, validity):

    def one_section(section):
        section_image = lax.dynamic_index_in_dim(pixels, section, 0, keepdims=False)
        earlier_image = lax.dynamic_index_in_dim(pixels, jnp.maximum(section - 1, 0), 0, keepdims=False)
        earlier_image = jnp.where(section > 0, earlier_image, jnp.zeros_like(earlier_image))
        offsets = lax.dynamic_index_in_dim(peak_offsets, section, 0, keepdims=False)

        def one_strip(strip_index):
            start = (strip_index * PATCH).astype(jnp.int32)
            strip_now = lax.dynamic_slice_in_dim(section_image, start, PATCH, 0)
            strip_old = lax.dynamic_slice_in_dim(earlier_image, start, PATCH, 0)
            strip_offsets = lax.dynamic_index_in_dim(offsets, strip_index, 1, keepdims=False)
            return refine(strip_spectrum(strip_now), strip_spectrum(strip_old), strip_offsets)
        strips = lax.map(one_strip, jnp.arange(NR, dtype=jnp.int32))
        return jnp.transpose(strips, (1, 0, 2))
    flow_field = lax.map(one_section, jnp.arange(SECTIONS, dtype=jnp.int32))
    mesh_field = relax(flow_field, validity)
    return (flow_field, mesh_field)
```

```python
import functools
import math

import jax
import jax.numpy as jnp
import ml_dtypes
import numpy as np
from jax import lax
from jax.experimental import pallas as pl
from jax.experimental.pallas import tpu as pltpu
from jax.sharding import PartitionSpec as P

PATCH = 64
HALF = PATCH // 2
RELAX = 8
GROUP = 8
CHUNK = GROUP * PATCH
SIDE = GROUP * HALF

spring_plane = 0.5
spring_stack = 1.0
step_size = 0.2
damping = 0.6
whiten_floor = 1024.0

MESH = pl.DeviceIdType.MESH
f32 = jnp.float32
bf16 = jnp.bfloat16


def cosine(m):
    angle = (np.asarray(m) % PATCH).astype(np.float32) * np.float32(2.0 * math.pi / PATCH)
    return np.cos(angle).astype(np.float32).astype(ml_dtypes.bfloat16).astype(np.float32)


def sine(m):
    angle = (np.asarray(m) % PATCH).astype(np.float32) * np.float32(2.0 * math.pi / PATCH)
    return np.sin(angle).astype(np.float32).astype(ml_dtypes.bfloat16).astype(np.float32)


@functools.lru_cache(maxsize=None)
def tables(patch_rows, patch_cols):
    y = np.arange(PATCH)
    k2 = np.arange(1, HALF + 1)
    col = np.zeros((4, PATCH, 2, 4, HALF), np.float32)
    for j in range(4):
        col[j, :, 0, j] = cosine(y[:, None] * k2)
        col[j, :, 1, j] = -sine(y[:, None] * k2)
    col = col.reshape(4 * PATCH, 8 * HALF)
    lanes = np.arange(patch_rows * patch_cols)
    zero = (np.arange(patch_cols * PATCH)[:, None] // PATCH == lanes % patch_cols).astype(np.float32)
    c = cosine(y[:, None] * y)
    s = sine(y[:, None] * y)
    row = np.block([[c, s], [-s, c]])
    row0 = np.concatenate([c, -s], 0)
    shift = np.arange(-3, 4)
    first = np.zeros((16, 2 * PATCH), np.float32)
    first[:7] = np.concatenate([cosine(shift[:, None] * y), -sine(shift[:, None] * y)], 1)
    first[8:15] = np.concatenate([sine(shift[:, None] * y), cosine(shift[:, None] * y)], 1)
    weight = np.where(k2 == HALF, 1.0, 2.0) / PATCH
    second = np.zeros((patch_cols // GROUP, 2, GROUP, HALF, 8, patch_cols), np.float32)
    for patch in range(patch_cols):
        at, j = divmod(patch, GROUP)
        second[at, 0, j, :, :7, patch] = weight[:, None] * cosine(k2[:, None] * shift)
        second[at, 1, j, :, :7, patch] = -weight[:, None] * sine(k2[:, None] * shift)
    second = second.reshape(patch_cols * PATCH, 8 * patch_cols)
    direct = np.zeros((lanes.size, 8, patch_cols), np.float32)
    direct[lanes, :7, lanes % patch_cols] = 1.0 / PATCH
    second = np.concatenate([second, direct.reshape(lanes.size, -1)], 0)
    return [t.astype(ml_dtypes.bfloat16) for t in (col, zero, row, row0, first, second)]


def dot(a, b):
    return jnp.dot(a, b, preferred_element_type=f32)


def whitened(now, old):
    now, old = now.astype(f32), old.astype(f32)
    now_real, now_imag = now[:PATCH], now[PATCH:]
    old_real, old_imag = old[:PATCH], old[PATCH:]
    cross_real = now_real * old_real + now_imag * old_imag
    cross_imag = now_imag * old_real - now_real * old_imag
    inverse = lax.rsqrt(
        cross_real * cross_real + cross_imag * cross_imag + whiten_floor * whiten_floor
    )
    return jnp.concatenate([cross_real * inverse, cross_imag * inverse], 0).astype(bf16)


def section_step(load, tabs, spec, spec0, sums, base, compare):
    col, zero, row, row0, first = [t[...] for t in tabs]
    patch_rows, unused, width = spec.shape
    chunks = width // SIDE
    lanes = spec0.shape[1]
    patch_cols = lanes // patch_rows
    totals = None
    for at in range(chunks):
        x = load(at)
        part = dot(x, zero[at * CHUNK:(at + 1) * CHUNK])
        totals = part if totals is None else totals + part
        halves = [
            dot(x[:, h * CHUNK // 2:(h + 1) * CHUNK // 2], col).astype(bf16) for h in range(2)
        ]
        real = jnp.concatenate([h[:, :SIDE // 2] for h in halves], 1)
        imag = jnp.concatenate([h[:, SIDE // 2:] for h in halves], 1)
        for a in range(patch_rows):
            part = slice(a * PATCH, (a + 1) * PATCH)
            now = dot(row, jnp.concatenate([real[part], imag[part]], 0)).astype(bf16)
            here = slice(at * SIDE, (at + 1) * SIDE)
            if compare:
                prod = whitened(now, spec[a, :, here])
                half = dot(first, prod)
                rows = pl.ds(base + a * 8, 8)
                sums[rows, at * CHUNK:at * CHUNK + SIDE] = half[:8]
                sums[rows, at * CHUNK + SIDE:(at + 1) * CHUNK] = half[8:]
            spec[a, :, here] = now
    lane = lax.broadcasted_iota(jnp.int32, (PATCH, lanes), 1) // patch_cols
    packed = jnp.zeros((PATCH, lanes), f32)
    for a in range(patch_rows):
        packed = jnp.where(lane == a, totals[a * PATCH:(a + 1) * PATCH], packed)
    now = dot(row0, packed.astype(bf16)).astype(bf16)
    if compare:
        half = dot(first, whitened(now, spec0[...]))[:8]
        for a in range(patch_rows):
            sums[pl.ds(base + a * 8, 8), chunks * CHUNK:] = jnp.where(lane[:8] == a, half, 0.0)
    spec0[...] = now


def pick(sums, second, peaks, patch_cols):
    corr = dot(sums.astype(bf16), second)
    count = corr.shape[0] // 8
    width = corr.shape[1]
    corr = corr.reshape(count, 8, width)
    p1, p2 = peaks[0], peaks[1]
    sub = lax.broadcasted_iota(jnp.int32, (count, 8, width), 1).astype(f32) - 3.0
    shift = lax.broadcasted_iota(jnp.int32, (count, width), 1) // patch_cols
    shift = shift.astype(f32) - 3.0
    p1_all = jnp.broadcast_to(p1[:, None, :], (count, 8, width))
    at1 = [jnp.sum(jnp.where(sub == p1_all + d, corr, 0.0), 1) for d in (-1.0, 0.0, 1.0)]

    def fold(values, d):
        values = jnp.where(shift == p2 + d, values, 0.0)
        reach = width // 2
        while reach >= patch_cols:
            values = values + pltpu.roll(values, reach, 1)
            reach //= 2
        return values

    center = fold(at1[1], 0.0)

    def step(low, high):
        return (low - high) / (2.0 * jnp.maximum(jnp.abs(low - 2.0 * center + high), 1.0))

    row_flow = p1 + step(fold(at1[0], 0.0), fold(at1[2], 0.0))
    col_flow = p2 + step(fold(at1[1], -1.0), fold(at1[1], 1.0))
    return row_flow, col_flow


def inner_kernel(count, pix, peaks, *refs):
    tabs, second, flow, spec, spec0, sums = refs[:5], refs[5], refs[6], refs[7], refs[8], refs[9]
    section = pl.program_id(0)
    patch_rows = spec.shape[0]
    patch_cols = spec0.shape[1] // patch_rows
    load = lambda at: pix[0, :, at * CHUNK:(at + 1) * CHUNK]

    @pl.when(section == 0)
    def _():
        section_step(load, tabs, spec, spec0, sums, 0, False)

    @pl.when(section > 0)
    def _():
        base = pl.multiple_of((section - 1) * patch_rows * 8, 8)
        section_step(load, tabs, spec, spec0, sums, base, True)

    @pl.when(section == count - 1)
    def _():
        flow[0], flow[1] = pick(sums[...], second[...], peaks, patch_cols)


def edge_kernel(top_old, low_old, top_now, low_now, peaks, *refs):
    tabs, second, flow, spec, spec0, sums = refs[:5], refs[5], refs[6], refs[7], refs[8], refs[9]
    patch_rows = spec.shape[0]
    patch_cols = spec0.shape[1] // patch_rows

    def pair(top, low):
        def load(at):
            here = slice(at * CHUNK, (at + 1) * CHUNK)
            return jnp.concatenate([top[0, :, here], low[0, :, here]], 0)
        return load

    section_step(pair(top_old, low_old), tabs, spec, spec0, sums, 0, False)
    section_step(pair(top_now, low_now), tabs, spec, spec0, sums, 0, True)
    flow[0], flow[1] = pick(sums[...], second[...], peaks, patch_cols)


def scratch(patch_rows, patch_cols, entries):
    return [
        pltpu.VMEM((patch_rows, 2 * PATCH, patch_cols * HALF), bf16),
        pltpu.VMEM((2 * PATCH, patch_rows * patch_cols), bf16),
        pltpu.VMEM((entries * 8, patch_cols * PATCH + patch_rows * patch_cols), f32),
    ]


def whole(array):
    return pl.BlockSpec(array.shape, lambda i: (0,) * array.ndim)


def inner_flow(pixels, peaks, tabs, patch_rows, patch_cols):
    count, height, width = pixels.shape
    entries = peaks.shape[1]
    return pl.pallas_call(
        functools.partial(inner_kernel, count),
        grid=(count,),
        in_specs=[pl.BlockSpec((1, height, width), lambda i: (i, 0, 0)), whole(peaks)]
        + [whole(t) for t in tabs],
        out_specs=pl.BlockSpec(peaks.shape, lambda i: (0, 0, 0)),
        out_shape=jax.ShapeDtypeStruct(peaks.shape, f32),
        scratch_shapes=scratch(patch_rows, patch_cols, entries),
        compiler_params=pltpu.CompilerParams(
            dimension_semantics=("arbitrary",), vmem_limit_bytes=32 * 1024 * 1024
        ),
        cost_estimate=pl.CostEstimate(
            flops=count * height * width * 2048, bytes_accessed=2 * pixels.size, transcendentals=0
        ),
        name="inner_flow",
    )(pixels, peaks, *tabs)


def edge_flow(pixels, from_last, from_next, peaks, tabs, patch_rows, patch_cols):
    count, height, width = pixels.shape
    block = (1, height // 2, width)
    return pl.pallas_call(
        edge_kernel,
        grid=(1,),
        in_specs=[
            pl.BlockSpec(block, lambda i: (0, 0, 0)),
            pl.BlockSpec(block, lambda i: (count - 1, 1, 0)),
            pl.BlockSpec(block, lambda i: (0, 0, 0)),
            pl.BlockSpec(block, lambda i: (0, 0, 0)),
            whole(peaks),
        ]
        + [whole(t) for t in tabs],
        out_specs=pl.BlockSpec(peaks.shape, lambda i: (0, 0, 0)),
        out_shape=jax.ShapeDtypeStruct(peaks.shape, f32),
        scratch_shapes=scratch(patch_rows, patch_cols, patch_rows),
        compiler_params=pltpu.CompilerParams(
            dimension_semantics=("arbitrary",), vmem_limit_bytes=32 * 1024 * 1024
        ),
        cost_estimate=pl.CostEstimate(
            flops=height * width * 4096, bytes_accessed=4 * height * width, transcendentals=0
        ),
        name="edge_flow",
    )(from_last, pixels, pixels, from_next, peaks, *tabs)


def gather_kernel(sizes, own, out, send, recv):
    size_x, size_y, size_s = sizes
    total = size_x * size_y * size_s
    me = (lax.axis_index("gx") * size_y + lax.axis_index("gy")) * size_s + lax.axis_index("sa")

    def place(i):
        there = lax.rem(me + i, total)
        return there // (size_y * size_s), lax.rem(there // size_s, size_y), lax.rem(there, size_s)

    barrier = pltpu.get_barrier_semaphore()

    @pl.loop(1, total)
    def _(i):
        pl.semaphore_signal(barrier, inc=1, device_id=place(i), device_id_type=MESH)

    pl.semaphore_wait(barrier, total - 1)

    def copy(i):
        return pltpu.make_async_remote_copy(
            src_ref=own,
            dst_ref=out.at[total - i],
            send_sem=send.at[i],
            recv_sem=recv.at[total - i],
            device_id=place(i),
            device_id_type=MESH,
        )

    @pl.loop(1, total)
    def _(i):
        copy(i).start()

    out[0] = own[...]

    @pl.loop(1, total)
    def _(i):
        copy(i).wait()


def gather(payload, sizes):
    total = math.prod(sizes)
    got = pl.pallas_call(
        functools.partial(gather_kernel, sizes),
        out_shape=jax.ShapeDtypeStruct((total,) + payload.shape, payload.dtype),
        in_specs=[pl.BlockSpec(memory_space=pltpu.VMEM)],
        out_specs=pl.BlockSpec(memory_space=pltpu.VMEM),
        scratch_shapes=[
            pltpu.SemaphoreType.DMA((total,)),
            pltpu.SemaphoreType.DMA((total,)),
        ],
        compiler_params=pltpu.CompilerParams(collective_id=0, has_side_effects=True),
        name="gather_flow",
    )(payload)
    me = (lax.axis_index("gx") * sizes[1] + lax.axis_index("gy")) * sizes[2] + lax.axis_index("sa")
    return jnp.roll(got, me, axis=0)


def edge_degree(row_index, col_index, total_rows, total_cols):
    return (
        4.0
        - (row_index == 0).astype(f32)
        - (row_index == total_rows - 1).astype(f32)
        - (col_index == 0).astype(f32)
        - (col_index == total_cols - 1).astype(f32)
    )


def relax_kernel(flow, weight, out, state):
    sections, parts, total_rows, total_cols = flow.shape
    w = weight[...][:, None]
    f = flow[...]
    running = f[0]
    state[0] = running
    for s in range(1, sections):
        running = running + f[s]
        state[s] = running
    row = lax.broadcasted_iota(jnp.int32, (total_rows, total_cols), 0)
    col = lax.broadcasted_iota(jnp.int32, (total_rows, total_cols), 1)
    degree = edge_degree(row, col, total_rows, total_cols)
    shape = (sections, parts, total_rows, total_cols)
    row4 = jnp.broadcast_to(row, shape)
    col4 = jnp.broadcast_to(col, shape)
    nothing = jnp.zeros((1,) + shape[1:], f32)
    w_next = jnp.concatenate([w[1:], jnp.zeros_like(w[:1])], 0)
    f_next = jnp.concatenate([f[1:], nothing], 0)

    def step(unused, carry):
        now, velocity = carry
        around = (
            jnp.where(row4 == 0, 0.0, pltpu.roll(now, 1, 2))
            + jnp.where(row4 == total_rows - 1, 0.0, pltpu.roll(now, total_rows - 1, 2))
            + jnp.where(col4 == 0, 0.0, pltpu.roll(now, 1, 3))
            + jnp.where(col4 == total_cols - 1, 0.0, pltpu.roll(now, total_cols - 1, 3))
        )
        lower = jnp.concatenate([nothing, now[:-1]], 0)
        upper = jnp.concatenate([now[1:], nothing], 0)
        here_term = w * (now - lower - f)
        next_term = w_next * (upper - now - f_next)
        gradient = spring_plane * (degree * now - around) + spring_stack * (here_term - next_term)
        velocity = damping * velocity - step_size * gradient
        return now + velocity, velocity

    final, unused_velocity = lax.fori_loop(
        0, RELAX, step, (state[...], jnp.zeros(shape, f32))
    )
    out[...] = final


def relax(flow, weight):
    return pl.pallas_call(
        relax_kernel,
        out_shape=jax.ShapeDtypeStruct(flow.shape, f32),
        in_specs=[pl.BlockSpec(memory_space=pltpu.VMEM)] * 2,
        out_specs=pl.BlockSpec(memory_space=pltpu.VMEM),
        scratch_shapes=[pltpu.VMEM(flow.shape, f32)],
        compiler_params=pltpu.CompilerParams(vmem_limit_bytes=32 * 1024 * 1024),
        name="relax",
    )(flow, weight)


def per_device(pixels, peak_offsets, validity):
    count, height, width = pixels.shape
    patch_rows, patch_cols = peak_offsets.shape[2:]
    half_rows = patch_rows // 2
    sizes = tuple(lax.axis_size(axis) for axis in ("gx", "gy", "sa"))
    size_x, size_y, size_s = sizes
    ahead = [(i, i + 1) for i in range(size_s - 1)]
    back = [(i + 1, i) for i in range(size_s - 1)]
    ring = [(i, (i - 1) % size_s) for i in range(size_s)]
    from_last = lax.ppermute(pixels[count - 1:, :height // 2], "sa", ahead)
    from_next = lax.ppermute(pixels[:1, height // 2:], "sa", back)
    peaks = peak_offsets.astype(f32)
    next_peaks = lax.ppermute(peaks[0, :, half_rows:], "sa", ring)
    edge_peaks = jnp.concatenate([peaks[0, :, :half_rows], next_peaks], 1)
    inner_peaks = jnp.transpose(peaks[1:], (1, 0, 2, 3)).reshape(2, -1, patch_cols)
    tabs = [jnp.asarray(t) for t in tables(patch_rows, patch_cols)]
    inner = inner_flow(pixels, jnp.tile(inner_peaks, (1, 1, 8)), tabs, patch_rows, patch_cols)
    edge = edge_flow(
        pixels, from_last, from_next, jnp.tile(edge_peaks, (1, 1, 8)), tabs, patch_rows, patch_cols
    )
    inner = inner[:, :, :patch_cols].reshape(2, count - 1, patch_rows * patch_cols)
    edge = edge[:, :, :patch_cols].reshape(2, 1, patch_rows * patch_cols)
    flows = jnp.concatenate([edge, inner], 1)
    weight = validity.astype(f32).reshape(1, count, patch_rows * patch_cols)
    payload = jnp.concatenate([flows, weight], 0).reshape(3 * count, patch_rows * patch_cols)
    everyone = gather(payload, sizes)
    blocks = everyone.reshape(size_x, size_y, size_s, 3, count, patch_rows, patch_cols)
    low = jnp.roll(blocks[:, :, :, :2, :1, half_rows:], 1, axis=2)
    low = jnp.concatenate([low, blocks[:, :, :, 2:, :1, half_rows:]], 3)
    begin = jnp.concatenate([blocks[:, :, :, :, :1, :half_rows], low], 5)
    blocks = jnp.concatenate([begin, blocks[:, :, :, :, 1:]], 4)
    blocks = jnp.transpose(blocks, (2, 4, 3, 1, 5, 0, 6))
    blocks = blocks.reshape(size_s * count, 3, size_y * patch_rows, size_x * patch_cols)
    all_flow, all_weight = blocks[:, :2], blocks[:, 2]
    final = relax(all_flow, all_weight)
    zero = jnp.zeros((), jnp.int32)
    starts = (
        lax.axis_index("sa") * count,
        zero,
        lax.axis_index("gy") * patch_rows,
        lax.axis_index("gx") * patch_cols,
    )
    shape = (count, 2, patch_rows, patch_cols)
    return lax.dynamic_slice(all_flow, starts, shape), lax.dynamic_slice(final, starts, shape)


def solution(mesh):
    return jax.shard_map(
        per_device,
        mesh=mesh,
        in_specs=(P("sa", "gy", "gx"), P("sa", None, "gy", "gx"), P("sa", "gy", "gx")),
        out_specs=(P("sa", None, "gy", "gx"), P("sa", None, "gy", "gx")),
        check_vma=False,
    )
```

```python
import functools
import math

import jax
import jax.numpy as jnp
import ml_dtypes
import numpy as np
from jax import lax
from jax.experimental import pallas as pl
from jax.experimental.pallas import tpu as pltpu
from jax.sharding import PartitionSpec as P

PATCH = 64
HALF = PATCH // 2
RELAX = 8
GROUP = 8
CHUNK = GROUP * PATCH
SIDE = GROUP * HALF

spring_plane = 0.5
spring_stack = 1.0
step_size = 0.2
damping = 0.6
whiten_floor = 1024.0

MESH = pl.DeviceIdType.MESH
f32 = jnp.float32
bf16 = jnp.bfloat16


def cosine(m):
    angle = (np.asarray(m) % PATCH).astype(np.float32) * np.float32(2.0 * math.pi / PATCH)
    return np.cos(angle).astype(np.float32).astype(ml_dtypes.bfloat16).astype(np.float32)


def sine(m):
    angle = (np.asarray(m) % PATCH).astype(np.float32) * np.float32(2.0 * math.pi / PATCH)
    return np.sin(angle).astype(np.float32).astype(ml_dtypes.bfloat16).astype(np.float32)


@functools.lru_cache(maxsize=None)
def tables(patch_rows, patch_cols):
    y = np.arange(PATCH)
    k2 = np.arange(1, HALF + 1)
    col = np.zeros((4, PATCH, 2, 4, HALF), np.float32)
    for j in range(4):
        col[j, :, 0, j] = cosine(y[:, None] * k2)
        col[j, :, 1, j] = -sine(y[:, None] * k2)
    col = col.reshape(4 * PATCH, 8 * HALF)
    lanes = np.arange(patch_rows * patch_cols)
    zero = (np.arange(patch_cols * PATCH)[:, None] // PATCH == lanes % patch_cols).astype(np.float32)
    c = cosine(y[:, None] * y)
    s = sine(y[:, None] * y)
    row = np.block([[c, s], [-s, c]])
    row0 = np.concatenate([c, -s], 0)
    shift = np.arange(-3, 4)
    first = np.zeros((16, 2 * PATCH), np.float32)
    first[:7] = np.concatenate([cosine(shift[:, None] * y), -sine(shift[:, None] * y)], 1)
    first[8:15] = np.concatenate([sine(shift[:, None] * y), cosine(shift[:, None] * y)], 1)
    weight = np.where(k2 == HALF, 1.0, 2.0) / PATCH
    second = np.zeros((patch_cols // GROUP, 2, GROUP, HALF, 8, patch_cols), np.float32)
    for patch in range(patch_cols):
        at, j = divmod(patch, GROUP)
        second[at, 0, j, :, :7, patch] = weight[:, None] * cosine(k2[:, None] * shift)
        second[at, 1, j, :, :7, patch] = -weight[:, None] * sine(k2[:, None] * shift)
    second = second.reshape(patch_cols * PATCH, 8 * patch_cols)
    direct = np.zeros((lanes.size, 8, patch_cols), np.float32)
    direct[lanes, :7, lanes % patch_cols] = 1.0 / PATCH
    second = np.concatenate([second, direct.reshape(lanes.size, -1)], 0)
    return [t.astype(ml_dtypes.bfloat16) for t in (col, zero, row, row0, first, second)]


def dot(a, b):
    return jnp.dot(a, b, preferred_element_type=f32)


def whitened(now, old):
    now, old = now.astype(f32), old.astype(f32)
    now_real, now_imag = now[:PATCH], now[PATCH:]
    old_real, old_imag = old[:PATCH], old[PATCH:]
    cross_real = now_real * old_real + now_imag * old_imag
    cross_imag = now_imag * old_real - now_real * old_imag
    inverse = lax.rsqrt(
        cross_real * cross_real + cross_imag * cross_imag + whiten_floor * whiten_floor
    )
    return jnp.concatenate([cross_real * inverse, cross_imag * inverse], 0).astype(bf16)


def section_step(load, tabs, spec, spec0, sums, base, mode, early=None, early0=None):
    col, zero, row, row0, first = [t[...] for t in tabs]
    patch_rows, unused, width = spec.shape
    chunks = width // SIDE
    lanes = spec0.shape[1]
    patch_cols = lanes // patch_rows
    upper = patch_rows // 2
    totals = None
    for at in range(chunks):
        x = load(at)
        part = dot(x, zero[at * CHUNK:(at + 1) * CHUNK])
        totals = part if totals is None else totals + part
        halves = [
            dot(x[:, h * CHUNK // 2:(h + 1) * CHUNK // 2], col).astype(bf16) for h in range(2)
        ]
        real = jnp.concatenate([h[:, :SIDE // 2] for h in halves], 1)
        imag = jnp.concatenate([h[:, SIDE // 2:] for h in halves], 1)
        here = slice(at * SIDE, (at + 1) * SIDE)
        for a in range(patch_rows):
            part = slice(a * PATCH, (a + 1) * PATCH)
            now = dot(row, jnp.concatenate([real[part], imag[part]], 0)).astype(bf16)
            if mode != "first":
                if mode == "edge" and a < upper:
                    prod = whitened(early[a, :, here], now)
                else:
                    prod = whitened(now, spec[a, :, here])
                half = dot(first, prod)
                rows = pl.ds(base + a * 8, 8)
                sums[rows, at * CHUNK:at * CHUNK + SIDE] = half[:8]
                sums[rows, at * CHUNK + SIDE:(at + 1) * CHUNK] = half[8:]
            if mode != "edge":
                spec[a, :, here] = now
            if mode == "first" and a < upper:
                early[a, :, here] = now
    lane = lax.broadcasted_iota(jnp.int32, (2 * PATCH, lanes), 1) // patch_cols
    packed = jnp.zeros((PATCH, lanes), f32)
    for a in range(patch_rows):
        packed = jnp.where(lane[:PATCH] == a, totals[a * PATCH:(a + 1) * PATCH], packed)
    now = dot(row0, packed.astype(bf16)).astype(bf16)
    if mode != "first":
        if mode == "edge":
            got = now.astype(f32)
            later = jnp.where(lane < upper, early0[...].astype(f32), got)
            before = jnp.where(lane < upper, got, spec0[...].astype(f32))
        else:
            later, before = now, spec0[...]
        half = dot(first, whitened(later, before))[:8]
        for a in range(patch_rows):
            sums[pl.ds(base + a * 8, 8), chunks * CHUNK:] = jnp.where(lane[:8] == a, half, 0.0)
    if mode != "edge":
        spec0[...] = now
    if mode == "first":
        early0[...] = now


def pick(sums, second, peaks, patch_cols):
    corr = dot(sums.astype(bf16), second)
    count = corr.shape[0] // 8
    width = corr.shape[1]
    corr = corr.reshape(count, 8, width)
    p1, p2 = peaks[0], peaks[1]
    sub = lax.broadcasted_iota(jnp.int32, (count, 8, width), 1).astype(f32) - 3.0
    shift = lax.broadcasted_iota(jnp.int32, (count, width), 1) // patch_cols
    shift = shift.astype(f32) - 3.0
    p1_all = jnp.broadcast_to(p1[:, None, :], (count, 8, width))
    at1 = [jnp.sum(jnp.where(sub == p1_all + d, corr, 0.0), 1) for d in (-1.0, 0.0, 1.0)]

    def fold(values, d):
        values = jnp.where(shift == p2 + d, values, 0.0)
        reach = width // 2
        while reach >= patch_cols:
            values = values + pltpu.roll(values, reach, 1)
            reach //= 2
        return values

    center = fold(at1[1], 0.0)

    def step(low, high):
        return (low - high) / (2.0 * jnp.maximum(jnp.abs(low - 2.0 * center + high), 1.0))

    row_flow = p1 + step(fold(at1[0], 0.0), fold(at1[2], 0.0))
    col_flow = p2 + step(fold(at1[1], -1.0), fold(at1[1], 1.0))
    return row_flow, col_flow


def packed_rows(flow, patch_rows, patch_cols):
    lanes = patch_rows * patch_cols
    flow = flow[:, :lanes].reshape(-1, patch_rows, lanes)
    lane = lax.broadcasted_iota(jnp.int32, flow.shape, 2) // patch_cols
    own = lax.broadcasted_iota(jnp.int32, flow.shape, 1)
    return jnp.sum(jnp.where(lane == own, flow, 0.0), 1)


def kernel(
    sizes, pixels, inner_peaks, top_peaks, low_peaks, weight,
    col_in, zero_in, row_in, row0_in, first_in, second_in,
    out,
    col, zero, row, row0, first, second,
    pix, edge, next_low, spec, spec0, early, early0, sums,
    message, edge_message, inbox, edge_inbox, flows, weights, state, speed,
    pix_sem, tab_sem, edge_send, edge_recv, msg_send, msg_recv, last_send, last_recv,
):
    size_x, size_y, size_s = sizes
    total = size_x * size_y * size_s
    my_x, my_y, my_s = lax.axis_index("gx"), lax.axis_index("gy"), lax.axis_index("sa")
    me = (my_x * size_y + my_y) * size_s + my_s
    count, height, width = pixels.shape
    patch_rows = spec.shape[0]
    lanes = spec0.shape[1]
    patch_cols = lanes // patch_rows
    upper = patch_rows // 2

    def place(i):
        there = lax.rem(me + i, total)
        return there // (size_y * size_s), lax.rem(there // size_s, size_y), lax.rem(there, size_s)

    barrier = pltpu.get_barrier_semaphore()

    @pl.loop(1, total)
    def _(i):
        pl.semaphore_signal(barrier, inc=1, device_id=place(i), device_id_type=MESH)

    pix_copies = [
        pltpu.make_async_copy(pixels.at[s], pix.at[s], pix_sem.at[s]) for s in range(count)
    ]
    tab_copies = [
        pltpu.make_async_copy(a, b, tab_sem.at[i])
        for i, (a, b) in enumerate(
            zip((col_in, zero_in, row_in, row0_in, first_in, second_in),
                (col, zero, row, row0, first, second))
        )
    ]
    pix_copies[0].start()
    for c in tab_copies[:5]:
        c.start()
    for c in pix_copies[1:]:
        c.start()
    tab_copies[5].start()

    half = height // 2
    ahead = pltpu.make_async_remote_copy(
        src_ref=pixels.at[count - 1, pl.ds(0, half)],
        dst_ref=edge.at[pl.ds(0, half)],
        send_sem=edge_send.at[0],
        recv_sem=edge_recv.at[0],
        device_id=(my_x, my_y, lax.rem(my_s + 1, size_s)),
        device_id_type=MESH,
    )
    back_to = (my_x, my_y, lax.rem(my_s + size_s - 1, size_s))
    back = pltpu.make_async_remote_copy(
        src_ref=pixels.at[0, pl.ds(half, half)],
        dst_ref=edge.at[pl.ds(half, half)],
        send_sem=edge_send.at[1],
        recv_sem=edge_recv.at[1],
        device_id=back_to,
        device_id_type=MESH,
    )
    peak_copy = pltpu.make_async_remote_copy(
        src_ref=low_peaks,
        dst_ref=next_low,
        send_sem=edge_send.at[2],
        recv_sem=edge_recv.at[2],
        device_id=back_to,
        device_id_type=MESH,
    )
    pl.semaphore_wait(barrier, total - 1)

    @pl.when(my_s < size_s - 1)
    def _():
        ahead.start()

    @pl.when(my_s > 0)
    def _():
        back.start()

    peak_copy.start()

    @pl.when(my_s == 0)
    def _():
        edge[:half] = jnp.zeros((half, width), bf16)

    @pl.when(my_s == size_s - 1)
    def _():
        edge[half:] = jnp.zeros((half, width), bf16)

    tabs = (col, zero, row, row0, first)
    for c in tab_copies[:5]:
        c.wait()
    for s in range(count):
        pix_copies[s].wait()
        if s == 0:
            section_step(
                lambda at: pix[0, :, at * CHUNK:(at + 1) * CHUNK],
                tabs, spec, spec0, sums, 0, "first", early, early0,
            )
    tab_copies[5].wait()

    @pl.loop(1, count)
    def _(s):
        section_step(
            lambda at: pix[s, :, at * CHUNK:(at + 1) * CHUNK],
            tabs, spec, spec0, sums, pl.multiple_of((s - 1) * patch_rows * 8, 8), "next",
        )

    inner = pick(sums[...], second[...], inner_peaks, patch_cols)
    for c in range(2):
        message[c, :1] = jnp.zeros((1, lanes), f32)
        message[c, 1:] = packed_rows(inner[c], patch_rows, patch_cols)
    message[2] = weight[...]
    inbox[my_x, my_y, my_s] = message[...]

    def sender(i, source, box, send, recv):
        return pltpu.make_async_remote_copy(
            src_ref=source,
            dst_ref=box.at[my_x, my_y, my_s],
            send_sem=send.at[i],
            recv_sem=recv.at[total - i],
            device_id=place(i),
            device_id_type=MESH,
        )

    def arrival(i, source, box, send, recv):
        x, y, s = place(i)
        return pltpu.make_async_remote_copy(
            src_ref=source,
            dst_ref=box.at[x, y, s],
            send_sem=send.at[i],
            recv_sem=recv.at[i],
            device_id=place(i),
            device_id_type=MESH,
        )

    inner_args = (message, inbox, msg_send, msg_recv)
    last_args = (edge_message, edge_inbox, last_send, last_recv)

    @pl.loop(1, total)
    def _(i):
        sender(i, *inner_args).start()

    @pl.when(my_s > 0)
    def _():
        ahead.wait_recv()

    @pl.when(my_s < size_s - 1)
    def _():
        back.wait_recv()

    peak_copy.wait_recv()
    section_step(
        lambda at: edge[:, at * CHUNK:(at + 1) * CHUNK],
        tabs, spec, spec0, sums, 0, "edge", early, early0,
    )
    edge_peaks = [jnp.concatenate([top_peaks[c], next_low[c]], 0) for c in range(2)]
    outer = pick(sums[:patch_rows * 8], second[...], edge_peaks, patch_cols)
    for c in range(2):
        edge_message[c:c + 1] = packed_rows(outer[c], patch_rows, patch_cols)
    edge_inbox[my_x, my_y, my_s] = edge_message[...]

    @pl.loop(1, total)
    def _(i):
        sender(i, *last_args).start()

    @pl.loop(1, total)
    def _(i):
        arrival(i, *inner_args).wait_recv()

    @pl.loop(1, total)
    def _(i):
        arrival(i, *last_args).wait_recv()

    sections = size_s * count
    total_rows, total_cols = size_y * patch_rows, size_x * patch_cols
    sub = lax.broadcasted_iota(jnp.int32, (sections, lanes), 0)
    lane = lax.broadcasted_iota(jnp.int32, (sections, lanes), 1)
    for y in range(size_y):
        for c in range(3):
            rows = [None] * patch_rows
            for x in range(size_x):
                block = jnp.concatenate([inbox[x, y, s, c] for s in range(size_s)], 0)
                if c < 2:
                    for s in range(size_s):
                        own = edge_inbox[x, y, s, c:c + 1]
                        before = edge_inbox[x, y, (s - 1) % size_s, c:c + 1]
                        begin = jnp.where(lane[:1] < upper * patch_cols, own, before)
                        block = jnp.where(sub == s * count, begin, block)
                for a in range(patch_rows):
                    turn = (x - a) * patch_cols % lanes
                    moved = pltpu.roll(block, turn, 1) if turn else block
                    if rows[a] is None:
                        rows[a] = moved
                    else:
                        rows[a] = jnp.where(lane // patch_cols == x, moved, rows[a])
            for a in range(patch_rows):
                if c < 2:
                    flows[c, y * patch_rows + a] = rows[a]
                else:
                    weights[y * patch_rows + a] = rows[a]

    def up(values):
        moved = pltpu.roll(values, sections - 1, values.ndim - 2)
        at = lax.broadcasted_iota(jnp.int32, values.shape, values.ndim - 2)
        return jnp.where(at == sections - 1, 0.0, moved)

    def down(values, by=1):
        moved = pltpu.roll(values, by, values.ndim - 2)
        at = lax.broadcasted_iota(jnp.int32, values.shape, values.ndim - 2)
        return jnp.where(at < by, 0.0, moved)

    running = flows[...]
    by = 1
    while by < sections:
        running = running + down(running, by)
        by *= 2
    state[0] = running
    speed[...] = jnp.zeros_like(running)
    first_col, last_col = lane == 0, lane == total_cols - 1
    ends = first_col.astype(f32) + last_col.astype(f32)

    for t in range(RELAX):
        now_at, then_at = t % 2, (t + 1) % 2

        @pl.loop(0, 2)
        def _(c):
            for r in range(total_rows):
                now = state[now_at, c, r]
                flow, w = flows[c, r], weights[r]
                around = jnp.where(first_col, 0.0, pltpu.roll(now, 1, 1)) + jnp.where(
                    last_col, 0.0, pltpu.roll(now, total_cols - 1, 1)
                )
                degree = 4.0 - ends
                if r > 0:
                    around = around + state[now_at, c, r - 1]
                else:
                    degree = degree - 1.0
                if r < total_rows - 1:
                    around = around + state[now_at, c, r + 1]
                else:
                    degree = degree - 1.0
                here_term = w * (now - down(now) - flow)
                next_term = up(here_term)
                gradient = spring_plane * (degree * now - around) + spring_stack * (
                    here_term - next_term
                )
                velocity = damping * speed[c, r] - step_size * gradient
                speed[c, r] = velocity
                state[then_at, c, r] = now + velocity

    where_s = my_s * count
    for field in range(2):
        for c in range(2):
            for a in range(patch_rows):
                r = my_y * patch_rows + a
                if field == 0:
                    values = flows[c, r, pl.ds(where_s, count)]
                else:
                    values = state[RELAX % 2, c, r, pl.ds(where_s, count)]
                mine = values
                for x in range(1, size_x):
                    moved = pltpu.roll(values, lanes - x * patch_cols, 1)
                    mine = jnp.where(my_x == x, moved, mine)
                out[field, c, a] = mine[:, :patch_cols]

    @pl.when(my_s < size_s - 1)
    def _():
        ahead.wait_send()

    @pl.when(my_s > 0)
    def _():
        back.wait_send()

    peak_copy.wait_send()

    @pl.loop(1, total)
    def _(i):
        sender(i, *inner_args).wait_send()

    @pl.loop(1, total)
    def _(i):
        sender(i, *last_args).wait_send()


def per_device(pixels, peak_offsets, validity):
    count, height, width = pixels.shape
    patch_rows, patch_cols = peak_offsets.shape[2:]
    lanes = patch_rows * patch_cols
    upper = patch_rows // 2
    sizes = tuple(lax.axis_size(axis) for axis in ("gx", "gy", "sa"))
    size_x, size_y, size_s = sizes
    total = math.prod(sizes)
    sections = size_s * count
    total_rows = size_y * patch_rows
    peaks = jnp.tile(peak_offsets.astype(f32), (1, 1, 1, 8))
    inner_peaks = jnp.transpose(peaks[1:], (1, 0, 2, 3)).reshape(2, -1, 8 * patch_cols)
    weight = validity.astype(f32).reshape(count, lanes)
    tabs = [jnp.asarray(t) for t in tables(patch_rows, patch_cols)]
    vmem = pl.BlockSpec(memory_space=pltpu.VMEM)
    anywhere = pl.BlockSpec(memory_space=pl.ANY)
    dma = pltpu.SemaphoreType.DMA
    plane = (sections, lanes)
    out = pl.pallas_call(
        functools.partial(kernel, sizes),
        in_specs=[anywhere] + [vmem] * 4 + [anywhere] * 6,
        out_specs=vmem,
        out_shape=jax.ShapeDtypeStruct((2, 2, patch_rows, count, patch_cols), f32),
        scratch_shapes=[pltpu.VMEM(t.shape, bf16) for t in tabs]
        + [
            pltpu.VMEM(pixels.shape, bf16),
            pltpu.VMEM((height, width), bf16),
            pltpu.VMEM((2, patch_rows - upper, 8 * patch_cols), f32),
            pltpu.VMEM((patch_rows, 2 * PATCH, patch_cols * HALF), bf16),
            pltpu.VMEM((2 * PATCH, lanes), bf16),
            pltpu.VMEM((upper, 2 * PATCH, patch_cols * HALF), bf16),
            pltpu.VMEM((2 * PATCH, lanes), bf16),
            pltpu.VMEM(((count - 1) * patch_rows * 8, patch_cols * PATCH + lanes), f32),
            pltpu.VMEM((3, count, lanes), f32),
            pltpu.VMEM((2, lanes), f32),
            pltpu.VMEM(sizes + (3, count, lanes), f32),
            pltpu.VMEM(sizes + (2, lanes), f32),
            pltpu.VMEM((2, total_rows) + plane, f32),
            pltpu.VMEM((total_rows,) + plane, f32),
            pltpu.VMEM((2, 2, total_rows) + plane, f32),
            pltpu.VMEM((2, total_rows) + plane, f32),
            dma((count,)),
            dma((6,)),
            dma((3,)),
            dma((3,)),
            dma((total,)),
            dma((total,)),
            dma((total,)),
            dma((total,)),
        ],
        compiler_params=pltpu.CompilerParams(
            collective_id=0, has_side_effects=True, vmem_limit_bytes=56 * 1024 * 1024
        ),
        name="align",
    )(pixels, inner_peaks, peaks[0, :, :upper], peaks[0, :, upper:], weight, *tabs)
    fields = jnp.transpose(out, (0, 3, 1, 2, 4))
    return fields[0], fields[1]


def solution(mesh):
    return jax.shard_map(
        per_device,
        mesh=mesh,
        in_specs=(P("sa", "gy", "gx"), P("sa", None, "gy", "gx"), P("sa", "gy", "gx")),
        out_specs=(P("sa", None, "gy", "gx"), P("sa", None, "gy", "gx")),
        check_vma=False,
    )
```

```python
import functools
import math

import jax
import jax.numpy as jnp
import ml_dtypes
import numpy as np
from jax import lax
from jax.experimental import pallas as pl
from jax.experimental.pallas import tpu as pltpu
from jax.sharding import PartitionSpec as P

PATCH = 64
HALF = PATCH // 2
RELAX = 8

spring_plane = 0.5
spring_stack = 1.0
step_size = 0.2
damping = 0.6
whiten_floor = 1024.0

MESH = pl.DeviceIdType.MESH
f32 = jnp.float32
bf16 = jnp.bfloat16


def cosine(m):
    angle = (np.asarray(m) % PATCH).astype(np.float32) * np.float32(2.0 * math.pi / PATCH)
    return np.cos(angle).astype(np.float32).astype(ml_dtypes.bfloat16).astype(np.float32)


def sine(m):
    angle = (np.asarray(m) % PATCH).astype(np.float32) * np.float32(2.0 * math.pi / PATCH)
    return np.sin(angle).astype(np.float32).astype(ml_dtypes.bfloat16).astype(np.float32)


@functools.lru_cache(maxsize=None)
def tables(patch_rows, patch_cols):
    y = np.arange(PATCH)
    k2 = np.arange(1, HALF + 1)
    col = np.zeros((4, PATCH, 2, 4, HALF), np.float32)
    for j in range(4):
        col[j, :, 0, j] = cosine(y[:, None] * k2)
        col[j, :, 1, j] = -sine(y[:, None] * k2)
    col = col.reshape(4 * PATCH, 8 * HALF)
    lanes = np.arange(patch_rows * patch_cols)
    zero = (np.arange(patch_cols * PATCH)[:, None] // PATCH == lanes % patch_cols).astype(np.float32)
    c = cosine(y[:, None] * y)
    s = sine(y[:, None] * y)
    row = np.block([[c, s], [-s, c]])
    row0 = np.concatenate([c, -s], 0)
    shift = np.arange(-3, 4)
    first = np.zeros((16, 2 * PATCH), np.float32)
    first[:7] = np.concatenate([cosine(shift[:, None] * y), -sine(shift[:, None] * y)], 1)
    first[8:15] = np.concatenate([sine(shift[:, None] * y), cosine(shift[:, None] * y)], 1)
    weight = np.where(k2 == HALF, 1.0, 2.0) / PATCH
    second = np.zeros((2, patch_cols, HALF, 8, patch_cols), np.float32)
    for patch in range(patch_cols):
        second[0, patch, :, :7, patch] = weight[:, None] * cosine(k2[:, None] * shift)
        second[1, patch, :, :7, patch] = -weight[:, None] * sine(k2[:, None] * shift)
    second = second.reshape(patch_cols * PATCH, 8 * patch_cols)
    direct = np.zeros((lanes.size, 8, patch_cols), np.float32)
    direct[lanes, :7, lanes % patch_cols] = 1.0 / PATCH
    second = np.concatenate([second, direct.reshape(lanes.size, -1)], 0)
    return [t.astype(ml_dtypes.bfloat16) for t in (col, zero, row, row0, first, second)]


def dot(a, b):
    return jnp.dot(a, b, preferred_element_type=f32)


def whitened(now, old):
    now, old = now.astype(f32), old.astype(f32)
    now_real, now_imag = now[:PATCH], now[PATCH:]
    old_real, old_imag = old[:PATCH], old[PATCH:]
    cross_real = now_real * old_real + now_imag * old_imag
    cross_imag = now_imag * old_real - now_real * old_imag
    inverse = lax.rsqrt(
        cross_real * cross_real + cross_imag * cross_imag + whiten_floor * whiten_floor
    )
    return jnp.concatenate([cross_real * inverse, cross_imag * inverse], 0).astype(bf16)


def section_step(x, tabs, spec, spec0, cols, sums, base, mode, early=None, early0=None):
    col, zero, row, row0, first = [t[...] for t in tabs]
    patch_rows, unused, width = spec.shape
    lanes = spec0.shape[1]
    patch_cols = lanes // patch_rows
    upper = patch_rows // 2
    group, out = 4 * PATCH, 4 * HALF
    for at in range(width // out):
        part = dot(x[:, at * group:(at + 1) * group], col).astype(bf16)
        here = slice(at * out, (at + 1) * out)
        for a in range(patch_rows):
            rows = slice(a * PATCH, (a + 1) * PATCH)
            cols[a, :PATCH, here] = part[rows, :out]
            cols[a, PATCH:, here] = part[rows, out:]
    totals = dot(x[...], zero)
    for a in range(patch_rows):
        now = dot(row, cols[a]).astype(bf16)
        if mode != "first":
            if mode == "edge" and a < upper:
                prod = whitened(early[a], now)
            else:
                prod = whitened(now, spec[a])
            half = dot(first, prod)
            rows = pl.ds(base + a * 8, 8)
            sums[rows, :width] = half[:8]
            sums[rows, width:2 * width] = half[8:]
        if mode != "edge":
            spec[a] = now
        if mode == "first" and a < upper:
            early[a] = now
    lane = lax.broadcasted_iota(jnp.int32, (2 * PATCH, lanes), 1) // patch_cols
    packed = jnp.zeros((PATCH, lanes), f32)
    for a in range(patch_rows):
        packed = jnp.where(lane[:PATCH] == a, totals[a * PATCH:(a + 1) * PATCH], packed)
    now = dot(row0, packed.astype(bf16)).astype(bf16)
    if mode != "first":
        if mode == "edge":
            got = now.astype(f32)
            later = jnp.where(lane < upper, early0[...].astype(f32), got)
            before = jnp.where(lane < upper, got, spec0[...].astype(f32))
        else:
            later, before = now, spec0[...]
        half = dot(first, whitened(later, before))[:8]
        for a in range(patch_rows):
            sums[pl.ds(base + a * 8, 8), 2 * width:] = jnp.where(lane[:8] == a, half, 0.0)
    if mode != "edge":
        spec0[...] = now
    if mode == "first":
        early0[...] = now


def pick(sums, second, peaks, patch_cols):
    corr = dot(sums.astype(bf16), second)
    count = corr.shape[0] // 8
    width = corr.shape[1]
    corr = corr.reshape(count, 8, width)
    p1, p2 = peaks[0], peaks[1]
    sub = lax.broadcasted_iota(jnp.int32, (count, 8, width), 1).astype(f32) - 3.0
    shift = lax.broadcasted_iota(jnp.int32, (count, width), 1) // patch_cols
    shift = shift.astype(f32) - 3.0
    p1_all = jnp.broadcast_to(p1[:, None, :], (count, 8, width))
    at1 = [jnp.sum(jnp.where(sub == p1_all + d, corr, 0.0), 1) for d in (-1.0, 0.0, 1.0)]

    def fold(values, d):
        values = jnp.where(shift == p2 + d, values, 0.0)
        reach = width // 2
        while reach >= patch_cols:
            values = values + pltpu.roll(values, reach, 1)
            reach //= 2
        return values

    center = fold(at1[1], 0.0)

    def step(low, high):
        return (low - high) / (2.0 * jnp.maximum(jnp.abs(low - 2.0 * center + high), 1.0))

    row_flow = p1 + step(fold(at1[0], 0.0), fold(at1[2], 0.0))
    col_flow = p2 + step(fold(at1[1], -1.0), fold(at1[1], 1.0))
    return row_flow, col_flow


def packed_rows(flow, patch_rows, patch_cols):
    lanes = patch_rows * patch_cols
    flow = flow[:, :lanes].reshape(-1, patch_rows, lanes)
    lane = lax.broadcasted_iota(jnp.int32, flow.shape, 2) // patch_cols
    own = lax.broadcasted_iota(jnp.int32, flow.shape, 1)
    return jnp.sum(jnp.where(lane == own, flow, 0.0), 1)


def kernel(
    sizes, pixels, peaks, validity,
    col_in, zero_in, row_in, row0_in, first_in, second_in,
    flow_out, mesh_out,
    col, zero, row, row0, first, second,
    pix, edge, next_peaks, spec, spec0, early, early0, cols, sums,
    message, edge_message, inbox, edge_inbox, flows, weights, state, speed,
    pix_sem, tab_sem, edge_send, edge_recv, msg_send, msg_recv, last_send, last_recv,
):
    size_x, size_y, size_s = sizes
    total = size_x * size_y * size_s
    my_x, my_y, my_s = lax.axis_index("gx"), lax.axis_index("gy"), lax.axis_index("sa")
    me = (my_x * size_y + my_y) * size_s + my_s
    count, height, width = pixels.shape
    patch_rows = spec.shape[0]
    lanes = spec0.shape[1]
    patch_cols = lanes // patch_rows
    upper = patch_rows // 2

    at_x = [lax.rem(my_x + d, size_x) for d in range(size_x)]
    at_y = [lax.rem(my_y + d, size_y) for d in range(size_y)]
    at_s = [lax.rem(my_s + d, size_s) for d in range(size_s)]
    others = [(x, y, s) for s in at_s for x in at_x for y in at_y][1:]

    barrier = pltpu.get_barrier_semaphore()
    for device in others:
        pl.semaphore_signal(barrier, inc=1, device_id=device, device_id_type=MESH)

    pix_copies = [
        pltpu.make_async_copy(pixels.at[s], pix.at[s], pix_sem.at[s]) for s in range(count)
    ]
    tab_copies = [
        pltpu.make_async_copy(a, b, tab_sem.at[i])
        for i, (a, b) in enumerate(
            zip((col_in, zero_in, row_in, row0_in, first_in, second_in),
                (col, zero, row, row0, first, second))
        )
    ]
    pix_copies[0].start()
    for c in tab_copies[:5]:
        c.start()
    for c in pix_copies[1:]:
        c.start()
    tab_copies[5].start()

    half = height // 2
    ahead = pltpu.make_async_remote_copy(
        src_ref=pixels.at[count - 1, pl.ds(0, half)],
        dst_ref=edge.at[pl.ds(0, half)],
        send_sem=edge_send.at[0],
        recv_sem=edge_recv.at[0],
        device_id=(my_x, my_y, lax.rem(my_s + 1, size_s)),
        device_id_type=MESH,
    )
    back_to = (my_x, my_y, lax.rem(my_s + size_s - 1, size_s))
    back = pltpu.make_async_remote_copy(
        src_ref=pixels.at[0, pl.ds(half, half)],
        dst_ref=edge.at[pl.ds(half, half)],
        send_sem=edge_send.at[1],
        recv_sem=edge_recv.at[1],
        device_id=back_to,
        device_id_type=MESH,
    )
    peak_copy = pltpu.make_async_remote_copy(
        src_ref=peaks.at[0],
        dst_ref=next_peaks,
        send_sem=edge_send.at[2],
        recv_sem=edge_recv.at[2],
        device_id=back_to,
        device_id_type=MESH,
    )
    pl.semaphore_wait(barrier, total - 1)

    @pl.when(my_s < size_s - 1)
    def _():
        ahead.start()

    @pl.when(my_s > 0)
    def _():
        back.start()

    peak_copy.start()

    @pl.when(my_s == 0)
    def _():
        edge[:half] = jnp.zeros((half, width), bf16)

    @pl.when(my_s == size_s - 1)
    def _():
        edge[half:] = jnp.zeros((half, width), bf16)

    tabs = (col, zero, row, row0, first)
    for c in tab_copies[:5]:
        c.wait()
    for s in range(count):
        pix_copies[s].wait()
        if s == 0:
            section_step(
                pix.at[0], tabs, spec, spec0, cols, sums, 0, "first", early, early0
            )
    tab_copies[5].wait()

    @pl.loop(1, count)
    def _(s):
        section_step(
            pix.at[s], tabs, spec, spec0, cols, sums,
            pl.multiple_of((s - 1) * patch_rows * 8, 8), "next",
        )

    repeat = (patch_cols, 8 * patch_cols)
    spread = (
        lax.broadcasted_iota(jnp.int32, repeat, 1) % patch_cols
        == lax.broadcasted_iota(jnp.int32, repeat, 0)
    ).astype(f32).astype(bf16)

    def repeated(blocks):
        return dot(jnp.concatenate([b.astype(f32) for b in blocks], 0).astype(bf16), spread)

    inner_peaks = [repeated([peaks[s, c] for s in range(1, count)]) for c in range(2)]
    weight = packed_rows(repeated([validity[s] for s in range(count)]), patch_rows, patch_cols)
    inner = pick(sums[...], second[...], inner_peaks, patch_cols)
    for c in range(2):
        message[c, :1] = jnp.zeros((1, lanes), f32)
        message[c, 1:] = packed_rows(inner[c], patch_rows, patch_cols)
    message[2] = weight
    inbox[me] = message[...]

    def push(source, box, send, recv):
        for device in others:
            pltpu.make_async_remote_copy(
                src_ref=source,
                dst_ref=box.at[me],
                send_sem=send,
                recv_sem=recv,
                device_id=device,
                device_id_type=MESH,
            ).start()

    def every(box, send, recv):
        return pltpu.make_async_remote_copy(
            src_ref=box.at[pl.ds(0, total - 1)],
            dst_ref=box.at[pl.ds(0, total - 1)],
            send_sem=send,
            recv_sem=recv,
            device_id=others[0],
            device_id_type=MESH,
        )

    push(message, inbox, msg_send, msg_recv)

    @pl.when(my_s > 0)
    def _():
        ahead.wait_recv()

    @pl.when(my_s < size_s - 1)
    def _():
        back.wait_recv()

    peak_copy.wait_recv()
    section_step(
        edge, tabs, spec, spec0, cols, sums, 0, "edge", early, early0
    )
    edge_peaks = [repeated([peaks[0, c, :upper], next_peaks[c, upper:]]) for c in range(2)]
    outer = pick(sums[:patch_rows * 8], second[...], edge_peaks, patch_cols)
    for c in range(2):
        edge_message[c:c + 1] = packed_rows(outer[c], patch_rows, patch_cols)
    edge_inbox[me] = edge_message[...]
    push(edge_message, edge_inbox, last_send, last_recv)
    every(inbox, msg_send, msg_recv).wait_recv()
    every(edge_inbox, last_send, last_recv).wait_recv()

    sections = size_s * count
    total_rows, total_cols = size_y * patch_rows, size_x * patch_cols
    sub = lax.broadcasted_iota(jnp.int32, (sections, lanes), 0)
    lane = lax.broadcasted_iota(jnp.int32, (sections, lanes), 1)
    for y in range(size_y):
        for c in range(3):
            rows = [None] * patch_rows
            for x in range(size_x):
                at = (x * size_y + y) * size_s
                block = jnp.concatenate([inbox[at + s, c] for s in range(size_s)], 0)
                if c < 2:
                    for s in range(size_s):
                        own = edge_inbox[at + s, c:c + 1]
                        before = edge_inbox[at + (s - 1) % size_s, c:c + 1]
                        begin = jnp.where(lane[:1] < upper * patch_cols, own, before)
                        block = jnp.where(sub == s * count, begin, block)
                for a in range(patch_rows):
                    turn = (x - a) * patch_cols % lanes
                    moved = pltpu.roll(block, turn, 1) if turn else block
                    if rows[a] is None:
                        rows[a] = moved
                    else:
                        rows[a] = jnp.where(lane // patch_cols == x, moved, rows[a])
            for a in range(patch_rows):
                if c < 2:
                    flows[c, y * patch_rows + a] = rows[a]
                else:
                    weights[y * patch_rows + a] = rows[a]

    def up(values):
        moved = pltpu.roll(values, sections - 1, values.ndim - 2)
        at = lax.broadcasted_iota(jnp.int32, values.shape, values.ndim - 2)
        return jnp.where(at == sections - 1, 0.0, moved)

    def down(values, by=1):
        moved = pltpu.roll(values, by, values.ndim - 2)
        at = lax.broadcasted_iota(jnp.int32, values.shape, values.ndim - 2)
        return jnp.where(at < by, 0.0, moved)

    running = flows[...]
    by = 1
    while by < sections:
        running = running + down(running, by)
        by *= 2
    state[0] = running
    speed[...] = jnp.zeros_like(running)
    first_col, last_col = lane == 0, lane == total_cols - 1
    ends = first_col.astype(f32) + last_col.astype(f32)

    for t in range(RELAX):
        now_at, then_at = t % 2, (t + 1) % 2

        @pl.loop(0, 2)
        def _(c):
            for r in range(total_rows):
                now = state[now_at, c, r]
                flow, w = flows[c, r], weights[r]
                around = jnp.where(first_col, 0.0, pltpu.roll(now, 1, 1)) + jnp.where(
                    last_col, 0.0, pltpu.roll(now, total_cols - 1, 1)
                )
                degree = 4.0 - ends
                if r > 0:
                    around = around + state[now_at, c, r - 1]
                else:
                    degree = degree - 1.0
                if r < total_rows - 1:
                    around = around + state[now_at, c, r + 1]
                else:
                    degree = degree - 1.0
                here_term = w * (now - down(now) - flow)
                next_term = up(here_term)
                gradient = spring_plane * (degree * now - around) + spring_stack * (
                    here_term - next_term
                )
                velocity = damping * speed[c, r] - step_size * gradient
                speed[c, r] = velocity
                state[then_at, c, r] = now + velocity

    where_s = my_s * count
    for field in range(2):
        for c in range(2):
            for a in range(patch_rows):
                r = my_y * patch_rows + a
                if field == 0:
                    values = flows[c, r, pl.ds(where_s, count)]
                else:
                    values = state[RELAX % 2, c, r, pl.ds(where_s, count)]
                mine = values
                for x in range(1, size_x):
                    moved = pltpu.roll(values, lanes - x * patch_cols, 1)
                    mine = jnp.where(my_x == x, moved, mine)
                out = mesh_out if field else flow_out
                for s in range(count):
                    out[s, c, a:a + 1] = mine[s:s + 1, :patch_cols]

    @pl.when(my_s < size_s - 1)
    def _():
        ahead.wait_send()

    @pl.when(my_s > 0)
    def _():
        back.wait_send()

    peak_copy.wait_send()

    every(inbox, msg_send, msg_recv).wait_send()
    every(edge_inbox, last_send, last_recv).wait_send()


def per_device(pixels, peak_offsets, validity):
    count, height, width = pixels.shape
    patch_rows, patch_cols = peak_offsets.shape[2:]
    lanes = patch_rows * patch_cols
    upper = patch_rows // 2
    sizes = tuple(lax.axis_size(axis) for axis in ("gx", "gy", "sa"))
    size_x, size_y, size_s = sizes
    total = math.prod(sizes)
    sections = size_s * count
    total_rows = size_y * patch_rows
    tabs = [jnp.asarray(t) for t in tables(patch_rows, patch_cols)]
    vmem = pl.BlockSpec(memory_space=pltpu.VMEM)
    anywhere = pl.BlockSpec(memory_space=pl.ANY)
    dma = pltpu.SemaphoreType.DMA
    plane = (sections, lanes)
    shape = jax.ShapeDtypeStruct(peak_offsets.shape, f32)
    return pl.pallas_call(
        functools.partial(kernel, sizes),
        in_specs=[anywhere] + [vmem] * 2 + [anywhere] * 6,
        out_specs=(vmem, vmem),
        out_shape=(shape, shape),
        scratch_shapes=[pltpu.VMEM(t.shape, bf16) for t in tabs]
        + [
            pltpu.VMEM(pixels.shape, bf16),
            pltpu.VMEM((height, width), bf16),
            pltpu.VMEM(peak_offsets.shape[1:], jnp.int32),
            pltpu.VMEM((patch_rows, 2 * PATCH, patch_cols * HALF), bf16),
            pltpu.VMEM((2 * PATCH, lanes), bf16),
            pltpu.VMEM((upper, 2 * PATCH, patch_cols * HALF), bf16),
            pltpu.VMEM((2 * PATCH, lanes), bf16),
            pltpu.VMEM((patch_rows, 2 * PATCH, patch_cols * HALF), bf16),
            pltpu.VMEM(((count - 1) * patch_rows * 8, patch_cols * PATCH + lanes), f32),
            pltpu.VMEM((3, count, lanes), f32),
            pltpu.VMEM((2, lanes), f32),
            pltpu.VMEM((total, 3, count, lanes), f32),
            pltpu.VMEM((total, 2, lanes), f32),
            pltpu.VMEM((2, total_rows) + plane, f32),
            pltpu.VMEM((total_rows,) + plane, f32),
            pltpu.VMEM((2, 2, total_rows) + plane, f32),
            pltpu.VMEM((2, total_rows) + plane, f32),
            dma((count,)),
            dma((6,)),
            dma((3,)),
            dma((3,)),
            dma,
            dma,
            dma,
            dma,
        ],
        compiler_params=pltpu.CompilerParams(
            collective_id=0, has_side_effects=True, vmem_limit_bytes=56 * 1024 * 1024
        ),
        name="align",
    )(pixels, peak_offsets, validity, *tabs)


def solution(mesh):
    return jax.shard_map(
        per_device,
        mesh=mesh,
        in_specs=(P("sa", "gy", "gx"), P("sa", None, "gy", "gx"), P("sa", "gy", "gx")),
        out_specs=(P("sa", None, "gy", "gx"), P("sa", None, "gy", "gx")),
        check_vma=False,
    )
```
